256 devices in a mesh: fsdp: 4 (over y), tp: 64 (over z, x, core).
Axes of the slice: x: 4, y: 4, z: 8, core: 2. Of those that a mesh axis runs over, the one named last changes fastest.
Arguments:
- tokens: bfloat16 [512, 8192], P('tp', 'fsdp'), may hold values from -6 to 6
- gate_weight: bfloat16 [8192, 28672], P('fsdp', 'tp'), may hold values from -0.09375 to 0.09375
- up_weight: bfloat16 [8192, 28672], P('fsdp', 'tp'), may hold values from -0.09375 to 0.09375
- down_weight: bfloat16 [28672, 8192], P('tp', 'fsdp'), may hold values from -0.0625 to 0.0625
- gate_mask: int32 [128, 448], P('fsdp', 'tp'), may hold values 0 or 1
- up_mask: int32 [128, 448], P('fsdp', 'tp'), may hold values 0 or 1
- down_mask: int32 [448, 128], P('tp', 'fsdp'), may hold values 0 or 1
- grad_out: bfloat16 [512, 8192], P('tp', 'fsdp'), may hold values from -6 to 6
Outputs:
- output: bfloat16 [512, 8192], P('tp', 'fsdp')
- grad_tokens: bfloat16 [512, 8192], P('tp', 'fsdp')
- grad_gate: bfloat16 [8192, 28672], P('fsdp', 'tp')
- grad_up: bfloat16 [8192, 28672], P('fsdp', 'tp')
- grad_down: bfloat16 [28672, 8192], P('tp', 'fsdp')
The draws below stay inside these ranges and needn't reach their ends.
All inputs are finite; a program needn't handle non-finite values. No bound on the sum of `gate_mask` or of `up_mask` or of `down_mask` on one device may be relied on, other than what follows from the above.
Results may differ from the reference program's by a relative error of at most 0.0049.
Values may be sent and summed in bfloat16 or wider, within the bound.
A program may use at most 128 MiB of HBM per device.

```python
import jax
import jax.numpy as jnp

D = 8192
FF = 28672
BLOCK = 64
TOKENS = 512


def touch_ends(drawn, own_key, low, top_value):
    dims = drawn.shape
    index_at = [jax.random.randint(jax.random.fold_in(own_key, axis), (), 0, dims[axis]) for axis in range(len(dims))]
    drawn = drawn.at[tuple(index_at)].set(low)
    longest = dims.index(max(dims))
    index_at[longest] = (index_at[longest] + 1) % dims[longest]
    return drawn.at[tuple(index_at)].set(top_value)


def block_scale(own_key, extent, shards, least, largest):
    gain = 1.0
    for dim, blocks in shards:
        heights = jax.random.uniform(jax.random.fold_in(jax.random.fold_in(own_key, 6), dim), (blocks,), jnp.float32, least / len(shards), largest / len(shards))
        gain = gain * jnp.repeat(jnp.exp(heights), extent[dim] // blocks).reshape((-1,) + (1,) * (len(extent) - 1 - dim))
    return gain


def noise(key, shape, spread, limit, split=(), kind=jnp.bfloat16):
    array = spread * jax.random.normal(key, shape, jnp.float32)
    if split:
        array = array * block_scale(key, shape, split, -0.22, 0.18)
    return jnp.clip(array, -limit, limit).astype(kind)


def setup_inputs(seed: int = 0) -> dict:
    key_of = jax.random.split(jax.random.key(seed), 9)
    tokens = noise(key_of[0], (TOKENS, D), 1.0, 6.0, ((0, 64), (1, 4)))
    gate_weight = noise(key_of[1], (D, FF), (D // 2) ** -0.5, 0.09375, ((0, 4), (1, 64)))
    up_weight = noise(key_of[2], (D, FF), (D // 2) ** -0.5, 0.09375, ((0, 4), (1, 64)))
    down_weight = noise(key_of[3], (FF, D), (FF // 4) ** -0.5, 0.0625, ((0, 64), (1, 4)))
    gate_mask = touch_ends((jax.random.randint(key_of[4], (D // BLOCK, FF // BLOCK), 0, 2) < 1).astype(jnp.int32), jax.random.fold_in(key_of[4], 1), 0, 1)
    up_mask = touch_ends((jax.random.randint(key_of[5], (D // BLOCK, FF // BLOCK), 0, 2) < 1).astype(jnp.int32), jax.random.fold_in(key_of[5], 1), 0, 1)
    down_mask = touch_ends((jax.random.randint(key_of[6], (FF // BLOCK, D // BLOCK), 0, 2) < 1).astype(jnp.int32), jax.random.fold_in(key_of[6], 1), 0, 1)
    grad_out = noise(key_of[7], (TOKENS, D), 1.0, 6.0, ((0, 64), (1, 4)))
    return dict(tokens=tokens, gate_weight=gate_weight, up_weight=up_weight, down_weight=down_weight, gate_mask=gate_mask, up_mask=up_mask, down_mask=down_mask, grad_out=grad_out)


def expand(mask, dtype):
    return jnp.repeat(jnp.repeat(mask, BLOCK, axis=0), BLOCK, axis=1).astype(dtype)


def reference(tokens, gate_weight, up_weight, down_weight, gate_mask, up_mask, down_mask, grad_out):
    gate_full = expand(gate_mask, gate_weight.dtype)
    up_full = expand(up_mask, up_weight.dtype)
    down_full = expand(down_mask, down_weight.dtype)
    gate_kept = gate_weight * gate_full
    up_kept = up_weight * up_full
    down_kept = down_weight * down_full
    gate_value = jnp.dot(tokens, gate_kept, preferred_element_type=jnp.float32)
    up_value = jnp.dot(tokens, up_kept, preferred_element_type=jnp.float32)
    sigmoid_gate = jax.nn.sigmoid(gate_value)
    activated = gate_value * sigmoid_gate
    hidden = (activated * up_value).astype(jnp.bfloat16)
    output = jnp.dot(hidden, down_kept, preferred_element_type=jnp.float32).astype(jnp.bfloat16)
    grad_hidden = jnp.dot(grad_out, down_kept.T, preferred_element_type=jnp.float32)
    grad_gate_value = (grad_hidden * up_value * sigmoid_gate * (1.0 + gate_value * (1.0 - sigmoid_gate))).astype(jnp.bfloat16)
    grad_up_value = (grad_hidden * activated).astype(jnp.bfloat16)
    grad_down = (jnp.dot(hidden.T, grad_out, preferred_element_type=jnp.float32) * down_full).astype(jnp.bfloat16)
    grad_gate = (jnp.dot(tokens.T, grad_gate_value, preferred_element_type=jnp.float32) * gate_full).astype(jnp.bfloat16)
    grad_up = (jnp.dot(tokens.T, grad_up_value, preferred_element_type=jnp.float32) * up_full).astype(jnp.bfloat16)
    grad_tokens = (jnp.dot(grad_gate_value, gate_kept.T, preferred_element_type=jnp.float32)
                   + jnp.dot(grad_up_value, up_kept.T, preferred_element_type=jnp.float32)).astype(jnp.bfloat16)
    return output, grad_tokens, grad_gate, grad_up, grad_down
```

```python
import jax
import jax.numpy as jnp
from jax import lax
from jax.experimental import pallas as pl
from jax.experimental.pallas import tpu as pltpu
from jax.sharding import PartitionSpec as P

NY, NZ, NX = 4, 8, 4
BLOCK = 64
TOK = 512
DL = 2048
FL = 448
SLAB = FL // NY
QW = DL // 4
HW = DL // 2
F32 = jnp.float32
BF16 = jnp.bfloat16
MESH = pl.DeviceIdType.MESH
N_SEMS = 160


def nt(left, right):
    return lax.dot_general(left, right, (((1,), (1,)), ((), ())), preferred_element_type=F32)


def kernel(
    tok_ref, cot_ref, wg_hbm, wu_hbm, wd_hbm, mg_ref, mu_ref, md_ref,
    out_ref, gtok_ref, gg_hbm, gu_hbm, gd_hbm,
    w, mx, xk, exs, exr, pf, sb, rb, act, full, tr,
    own, psend, precv, xsend, xrecv, x2send, x2recv, ring_s, ring_r,
    r0, r1, zsend, zrecv, fin, finr, gout,
    send_sem, recv_sem, loc_sem,
):
    f = lax.axis_index("fsdp")
    t = lax.axis_index("tp")
    z = t // (2 * NX)
    x = (t // 2) % NX
    c = t % 2
    o = 1 - c

    def at(dy=0, dz=0, dx=0, flip=False):
        core = o if flip else c
        zz = lax.rem(z + dz + NZ, NZ)
        xx = lax.rem(x + dx + NX, NX)
        return (lax.rem(f + dy, NY), zz * (2 * NX) + xx * 2 + core)

    partner = at(flip=True)
    peers = [at(dy=d) for d in range(1, NY)]
    peers += [at(dz=d) for d in range(1, NZ)]
    peers += [at(dx=d) for d in range(1, NX)]
    peers += [partner]

    barrier = pltpu.get_barrier_semaphore()
    for peer in peers:
        pl.semaphore_signal(barrier, inc=1, device_id=peer, device_id_type=MESH)

    loads = [
        pltpu.make_async_copy(src, w.at[i], loc_sem.at[i])
        for i, src in enumerate((wg_hbm, wu_hbm, wd_hbm))
    ]
    for load in loads:
        load.start()

    for a, ref in enumerate((tok_ref, cot_ref)):
        exs[a] = ref[:, pl.ds(pl.multiple_of(o * HW, HW), HW)].astype(F32)
    pl.semaphore_wait(barrier, len(peers))

    sent = []

    def send(src, dst, peer):
        i = len(sent)
        copy = pltpu.make_async_remote_copy(
            src_ref=src, dst_ref=dst, send_sem=send_sem.at[i], recv_sem=recv_sem.at[i],
            device_id=peer, device_id_type=MESH,
        )
        copy.start()
        sent.append(copy)
        return copy

    def zr(d):
        return lax.rem(z + d + NZ, NZ)

    def xr(d):
        return lax.rem(x + d + NX, NX)

    exchange = [send(exs.at[a], exr.at[a], partner) for a in range(2)]
    k0, k1 = 2 * c, 2 * c + 1

    q0x, q1z = [], []
    for a, ref in enumerate((tok_ref, cot_ref)):
        exchange[a].wait_recv()
        mine = ref[:, pl.ds(pl.multiple_of(c * HW, HW), HW)].astype(F32)
        theirs = exr[a]
        first = jnp.where(c == 0, mine, theirs)
        second = jnp.where(c == 0, theirs, mine)
        rows = jnp.concatenate([first, second], axis=0).astype(BF16)
        xk[a, k0, z, x] = rows[:, :QW]
        xk[a, k1, z, x] = rows[:, QW:]
        here = xk.at[a, k0, z, x]
        q0x.append([send(here, here, at(dx=d)) for d in (1, 3, 2)])
    for a in range(2):
        here = xk.at[a, k1, z, x]
        q1z.append([send(here, here, at(dz=d)) for d in (1, 7, 2, 6, 3, 5, 4)])

    feature_block = lax.broadcasted_iota(jnp.int32, (DL // BLOCK, DL), 1) // BLOCK
    block = lax.broadcasted_iota(jnp.int32, (DL // BLOCK, DL), 0)
    spread = (feature_block == block).astype(F32).astype(BF16)
    for i, ref in enumerate((mg_ref, mu_ref, md_ref)):
        mx[i, 0 : FL // BLOCK] = jnp.dot(
            ref[...].astype(F32).astype(BF16), spread, preferred_element_type=F32
        )

    def prune(i):
        loads[i].wait()

        @pl.loop(0, FL // BLOCK)
        def _(b):
            rows = pl.ds(pl.multiple_of(b * BLOCK, BLOCK), BLOCK)
            w[i, rows, :] = (w[i, rows, :].astype(F32) * mx[i, pl.ds(b, 1), :]).astype(BF16)

    fwd = []

    def forward(ref):
        fwd.append(send(ref, ref, partner))

    up, down = [[], []], [[], []]
    for a in range(2):
        for copy in q0x[a]:
            copy.wait_recv()
        here = xk.at[a, k0, z]
        up[a].append(send(here, here, at(dz=1)))
        down[a].append(send(here, here, at(dz=-1)))
        forward(here)
    prune(0)
    q1x = []
    for a in range(2):
        for copy in q1z[a]:
            copy.wait_recv()
        here = xk.at[a, k1, :, x]
        q1x.append([send(here, here, at(dx=d)) for d in (1, 3, 2)])
        forward(here)
    for hop in (1, 2, 3):
        for a in range(2):
            up[a][hop - 1].wait_recv()
            got = xk.at[a, k0, zr(-hop)]
            part = got if hop < 3 else xk.at[a, k0, zr(-hop), 0:2]
            up[a].append(send(part, part, at(dz=1)))
            forward(got)
            down[a][hop - 1].wait_recv()
            got = xk.at[a, k0, zr(hop)]
            part = got if hop < 3 else xk.at[a, k0, zr(hop), 2:4]
            down[a].append(send(part, part, at(dz=-1)))
            forward(got)
        if hop < 3:
            prune(hop)
    for a in range(2):
        for copy, d in zip(q1x[a], (1, 3, 2)):
            copy.wait_recv()
            forward(xk.at[a, k1, :, xr(-d)])
    for a in range(2):
        up[a][3].wait_recv()
        forward(xk.at[a, k0, zr(4), 0:2])
        down[a][3].wait_recv()
        forward(xk.at[a, k0, zr(4), 2:4])
    for copy in fwd:
        copy.wait_recv()

    def project(m, a):
        @pl.loop(0, 4)
        def _(i):
            rows = pl.ds(pl.multiple_of((i // 2) * (FL // 2), FL // 2), FL // 2)
            cols = pl.ds(pl.multiple_of((i % 2) * 256, 256), 256)
            zs = pl.ds((i % 2) * 4, 4)
            total = None
            for k in range(4):
                term = nt(
                    w[m, rows, k * QW : (k + 1) * QW],
                    xk[a, k, zs].reshape(256, QW),
                )
                total = term if total is None else total + term
            pf[m, rows, cols] = total
            sb[m, rows, cols] = total.astype(BF16)

    def scatter(m):
        copies = []
        for d in (1, 3, 2):
            theirs = pl.ds(pl.multiple_of(lax.rem(f + d, NY) * SLAB, 16), SLAB)
            copies.append(send(sb.at[m, theirs, :], rb.at[m, d - 1], at(dy=d)))
        return copies

    my_slab = pl.multiple_of(f * SLAB, 16)
    sums = []
    for m, a in ((0, 0), (1, 0), (2, 1)):
        project(m, a)
        sums.append(scatter(m))

    def summed(m, b):
        rows = pl.ds(pl.multiple_of(b * 16, 16), 16)
        total = pf[m, pl.ds(pl.multiple_of(my_slab + b * 16, 16), 16), :]
        for d in range(3):
            total = total + rb[m, d, rows, :].astype(F32)
        return total

    def gather(i):
        here = full.at[i, pl.ds(my_slab, SLAB), :]
        return [send(here, here, at(dy=d)) for d in (1, 3, 2)]

    for m in range(2):
        for copy in sums[m]:
            copy.wait_recv()

    @pl.loop(0, SLAB // 16)
    def _(b):
        rows = pl.ds(pl.multiple_of(b * 16, 16), 16)
        gate = summed(0, b)
        upv = summed(1, b)
        sig = 1.0 / (1.0 + jnp.exp(-gate))
        activated = gate * sig
        full[0, pl.ds(pl.multiple_of(my_slab + b * 16, 16), 16), :] = (activated * upv).astype(BF16)
        act[0, rows, :] = activated
        act[1, rows, :] = upv * sig * (1.0 + gate * (1.0 - sig))

    hidden = gather(0)
    for copy in sums[2]:
        copy.wait_recv()

    @pl.loop(0, SLAB // 16)
    def _(b):
        rows = pl.ds(pl.multiple_of(b * 16, 16), 16)
        mine = pl.ds(pl.multiple_of(my_slab + b * 16, 16), 16)
        grad_hidden = summed(2, b)
        full[1, mine, :] = (grad_hidden * act[1, rows, :]).astype(BF16)
        full[2, mine, :] = (grad_hidden * act[0, rows, :]).astype(BF16)

    grads = [gather(1), gather(2)]

    def turn(i):
        @pl.loop(0, TOK // 128)
        def _(b):
            cols = pl.ds(pl.multiple_of(b * 128, 128), 128)
            tr[i, cols, :] = full[i, :, cols].astype(F32).T.astype(BF16)

    def product(a, pairs):
        copies = []
        for half, dst in ((o, psend), (c, own)):
            for j in range(2):

                @pl.loop(0, HW // 256)
                def _(n):
                    cols = pl.ds(pl.multiple_of(half * HW + n * 256, 256), 256)
                    total = None
                    for i, m in pairs:
                        term = jnp.dot(
                            tr[i, j * 256 : (j + 1) * 256, :], w[m, :, cols],
                            preferred_element_type=F32,
                        )
                        total = term if total is None else total + term
                    dst[a, j * 4 : (j + 1) * 4, :, :, pl.ds(pl.multiple_of(n * 256, 256), 256)] = (
                        total.reshape(4, NX, 16, 256)
                    )

                if dst is psend:
                    part = pl.ds(j * 4, 4)
                    copies.append(send(psend.at[a, part], precv.at[a, part], partner))
        return copies

    stores = []

    def weight_grad(i, a, m, hbm):
        @pl.loop(0, 4)
        def _(k):
            cols = pl.ds(pl.multiple_of(k * QW, QW), QW)
            total = jnp.dot(full[i], xk[a, k].reshape(TOK, QW), preferred_element_type=F32)
            for b in range(FL // BLOCK):
                rows = slice(b * BLOCK, (b + 1) * BLOCK)
                gout[m, rows, cols] = (total[rows] * mx[m, b : b + 1, cols]).astype(BF16)

        store = pltpu.make_async_copy(gout.at[m], hbm, loc_sem.at[3 + m])
        store.start()
        stores.append(store)

    for copy in hidden:
        copy.wait_recv()
    turn(0)
    swap = [product(0, ((0, 2),))]
    weight_grad(0, 1, 2, gd_hbm)
    for i in range(2):
        for copy in grads[i]:
            copy.wait_recv()
        turn(1 + i)
    swap.append(product(1, ((1, 0), (2, 1))))

    def part(a, zz, xs, q):
        cols = slice(q * QW, (q + 1) * QW)
        return own[a, zz, xs, :, cols] + precv[a, zz, xs, :, cols]

    up, down, bulk = [[], []], [[], []], []
    for a in range(2):
        for copy in swap[a]:
            copy.wait_recv()
        ring_s[a, 0, 0, 0:2] = part(a, zr(4), slice(0, 2), 0).astype(BF16)
        up[a].append(send(ring_s.at[a, 0, 0, 0:2], ring_r.at[a, 0, 0, 0:2], at(dz=1)))
        ring_s[a, 1, 0, 0:2] = part(a, zr(4), slice(2, 4), 0).astype(BF16)
        down[a].append(send(ring_s.at[a, 1, 0, 0:2], ring_r.at[a, 1, 0, 0:2], at(dz=-1)))
    for a in range(2):
        copies = []
        for d in (2, 1, 3):
            xsend[a, d - 1] = part(a, slice(0, NZ), xr(d), 1).astype(BF16)
            copies.append(send(xsend.at[a, d - 1], xrecv.at[a, d - 1], at(dx=d)))
        bulk.append(copies)

    def hop_on(a, hop):
        for side, chain, sign in ((0, up, 1), (1, down, -1)):
            chain[a][hop - 1].wait_recv()
            to = zr(sign * (4 - hop))
            if hop == 1:
                lo, hi = (slice(0, 2), slice(2, 4)) if side == 0 else (slice(2, 4), slice(0, 2))
                ring_s[a, side, hop, lo] = (
                    part(a, to, lo, 0) + ring_r[a, side, 0, 0:2].astype(F32)
                ).astype(BF16)
                ring_s[a, side, hop, hi] = part(a, to, hi, 0).astype(BF16)
            else:
                ring_s[a, side, hop] = (
                    part(a, to, slice(0, 4), 0) + ring_r[a, side, hop - 1].astype(F32)
                ).astype(BF16)
            chain[a].append(
                send(ring_s.at[a, side, hop], ring_r.at[a, side, hop], at(dz=sign))
            )

    for a in range(2):
        hop_on(a, 1)
    weight_grad(1, 0, 0, gg_hbm)
    for a in range(2):
        hop_on(a, 2)
    weight_grad(2, 0, 1, gu_hbm)
    for a in range(2):
        hop_on(a, 3)

    small = []
    for a in range(2):
        for copy in bulk[a]:
            copy.wait_recv()
        total = part(a, slice(0, NZ), x, 1)
        for d in range(3):
            total = total + xrecv[a, d].astype(F32)
        r1[a] = total
        copies = []
        for d in (4, 3, 5, 2, 6, 1, 7):
            zsend[a, d - 1] = r1[a, zr(d)].astype(BF16)
            copies.append(send(zsend.at[a, d - 1], zrecv.at[a, d - 1], at(dz=d)))
        small.append(copies)

    last = []
    for a in range(2):
        up[a][3].wait_recv()
        down[a][3].wait_recv()
        r0[a] = part(a, z, slice(0, 4), 0) + ring_r[a, 0, 3].astype(F32) + ring_r[a, 1, 3].astype(F32)
        copies = []
        for d in (2, 1, 3):
            x2send[a, d - 1] = r0[a, xr(d)].astype(BF16)
            copies.append(send(x2send.at[a, d - 1], x2recv.at[a, d - 1], at(dx=d)))
        last.append(copies)

    final = []
    for a in range(2):
        for copy in last[a]:
            copy.wait_recv()
        total0 = r0[a, x]
        for d in range(3):
            total0 = total0 + x2recv[a, d].astype(F32)
        for copy in small[a]:
            copy.wait_recv()
        total1 = r1[a, z]
        for d in range(7):
            total1 = total1 + zrecv[a, d].astype(F32)
        fin[a, :, :, :QW] = total0.reshape(2, 8, QW)
        fin[a, :, :, QW:] = total1.reshape(2, 8, QW)
        final.append(send(fin.at[a, o], finr.at[a], partner))
    for a, ref in enumerate((out_ref, gtok_ref)):
        final[a].wait_recv()
        ref[:, pl.ds(pl.multiple_of(c * HW, HW), HW)] = fin[a, c].astype(BF16)
        ref[:, pl.ds(pl.multiple_of(o * HW, HW), HW)] = finr[a].astype(BF16)

    for copy in sent:
        copy.wait_send()
    for store in stores:
        store.wait()


def body(tokens, gate_weight, up_weight, down_weight, gate_mask, up_mask, down_mask, grad_out):
    vmem = pl.BlockSpec(memory_space=pltpu.VMEM)
    hbm = pl.BlockSpec(memory_space=pl.ANY)
    out, gtok, gg, gu, gd = pl.pallas_call(
        kernel,
        name="ffn",
        out_shape=(
            jax.ShapeDtypeStruct((8, DL), BF16),
            jax.ShapeDtypeStruct((8, DL), BF16),
            jax.ShapeDtypeStruct((FL, DL), BF16),
            jax.ShapeDtypeStruct((FL, DL), BF16),
            jax.ShapeDtypeStruct((FL, DL), BF16),
        ),
        in_specs=[vmem, vmem, hbm, hbm, hbm, vmem, vmem, vmem],
        out_specs=(vmem, vmem, hbm, hbm, hbm),
        scratch_shapes=[
            pltpu.VMEM((3, FL, DL), BF16),
            pltpu.VMEM((3, 8, DL), F32),
            pltpu.VMEM((2, 4, NZ, NX, 16, QW), BF16),
            pltpu.VMEM((2, 8, HW), F32),
            pltpu.VMEM((2, 8, HW), F32),
            pltpu.VMEM((3, FL, TOK), F32),
            pltpu.VMEM((3, FL, TOK), BF16),
            pltpu.VMEM((3, 3, SLAB, TOK), BF16),
            pltpu.VMEM((2, SLAB, TOK), F32),
            pltpu.VMEM((3, FL, TOK), BF16),
            pltpu.VMEM((3, TOK, FL), BF16),
            pltpu.VMEM((2, NZ, NX, 16, HW), F32),
            pltpu.VMEM((2, NZ, NX, 16, HW), F32),
            pltpu.VMEM((2, NZ, NX, 16, HW), F32),
            pltpu.VMEM((2, 3, NZ, 16, QW), BF16),
            pltpu.VMEM((2, 3, NZ, 16, QW), BF16),
            pltpu.VMEM((2, 3, 16, QW), BF16),
            pltpu.VMEM((2, 3, 16, QW), BF16),
            pltpu.VMEM((2, 2, 4, NX, 16, QW), BF16),
            pltpu.VMEM((2, 2, 4, NX, 16, QW), BF16),
            pltpu.VMEM((2, NX, 16, QW), F32),
            pltpu.VMEM((2, NZ, 16, QW), F32),
            pltpu.VMEM((2, 7, 16, QW), BF16),
            pltpu.VMEM((2, 7, 16, QW), BF16),
            pltpu.VMEM((2, 2, 8, HW), F32),
            pltpu.VMEM((2, 8, HW), F32),
            pltpu.VMEM((3, FL, DL), BF16),
            pltpu.SemaphoreType.DMA((N_SEMS,)),
            pltpu.SemaphoreType.DMA((N_SEMS,)),
            pltpu.SemaphoreType.DMA((6,)),
        ],
        compiler_params=pltpu.CompilerParams(
            collective_id=0, has_side_effects=True, vmem_limit_bytes=56 * 2**20
        ),
    )(
        tokens, grad_out, gate_weight.T, up_weight.T, down_weight,
        gate_mask.T, up_mask.T, down_mask,
    )
    return out, gtok, gg.T, gu.T, gd


def solution(mesh):
    placed = (
        P("tp", "fsdp"),
        P("fsdp", "tp"),
        P("fsdp", "tp"),
        P("tp", "fsdp"),
        P("fsdp", "tp"),
        P("fsdp", "tp"),
        P("tp", "fsdp"),
        P("tp", "fsdp"),
    )
    return jax.shard_map(
        body,
        mesh=mesh,
        in_specs=placed,
        out_specs=(
            P("tp", "fsdp"),
            P("tp", "fsdp"),
            P("fsdp", "tp"),
            P("fsdp", "tp"),
            P("tp", "fsdp"),
        ),
        check_vma=False,
    )
```

```python
import jax
import jax.numpy as jnp
from jax import lax
from jax.experimental import pallas as pl
from jax.experimental.pallas import tpu as pltpu
from jax.sharding import PartitionSpec as P

NY, NZ, NX = 4, 8, 4
BLOCK = 64
TOK = 512
DL = 2048
FL = 448
SLAB = FL // NY
QW = DL // 4
HW = DL // 2
F32 = jnp.float32
BF16 = jnp.bfloat16
MESH = pl.DeviceIdType.MESH
N_SEMS = 160
VMEM = 57 * 2**20


def nt(left, right):
    return lax.dot_general(left, right, (((1,), (1,)), ((), ())), preferred_element_type=F32)


def kernel(
    tok_hbm, cot_hbm, wg_hbm, wu_hbm, wd_hbm, mg_hbm, mu_hbm, md_hbm,
    out_ref, gtok_ref, gg_hbm, gu_hbm, gd_hbm,
    rows_in, masks_in, w, mx, xk, exs, exr, pf, sb, rb, act, full, tr,
    own, psend, precv, xsend, xrecv, x2send, x2recv, ring_s, ring_r,
    r0, r1, zsend, zrecv, fin, finr, gout,
    send_sem, recv_sem, loc_sem,
):
    f = lax.axis_index("fsdp")
    t = lax.axis_index("tp")
    z = t // (2 * NX)
    x = (t // 2) % NX
    c = t % 2
    o = 1 - c

    def at(dy=0, dz=0, dx=0, flip=False):
        core = o if flip else c
        zz = lax.rem(z + dz + NZ, NZ)
        xx = lax.rem(x + dx + NX, NX)
        return (lax.rem(f + dy + NY, NY), zz * (2 * NX) + xx * 2 + core)

    partner = at(flip=True)
    peers = [at(dy=d) for d in range(1, NY)]
    peers += [at(dz=d) for d in range(1, NZ)]
    peers += [at(dx=d) for d in range(1, NX)]
    peers += [partner]

    barrier = pltpu.get_barrier_semaphore()
    for peer in peers:
        pl.semaphore_signal(barrier, inc=1, device_id=peer, device_id_type=MESH)

    tokens_in = [
        pltpu.make_async_copy(src, rows_in.at[a], loc_sem.at[6 + a])
        for a, src in enumerate((tok_hbm, cot_hbm))
    ]
    blocks_in = [
        pltpu.make_async_copy(src, masks_in.at[i], loc_sem.at[8 + i])
        for i, src in enumerate((mg_hbm, mu_hbm, md_hbm))
    ]
    loads = [
        pltpu.make_async_copy(src, w.at[i], loc_sem.at[i])
        for i, src in enumerate((wg_hbm, wu_hbm, wd_hbm))
    ]
    loads = tokens_in + blocks_in + loads
    for load in loads:
        load.start()

    for a in range(2):
        loads[a].wait()
        exs[a] = rows_in[a, :, pl.ds(pl.multiple_of(o * HW, HW), HW)].astype(F32)
    pl.semaphore_wait(barrier, len(peers))

    sent = []

    def send(src, dst, peer):
        i = len(sent)
        copy = pltpu.make_async_remote_copy(
            src_ref=src, dst_ref=dst, send_sem=send_sem.at[i], recv_sem=recv_sem.at[i],
            device_id=peer, device_id_type=MESH,
        )
        copy.start()
        sent.append(copy)
        return copy

    def zr(d):
        return lax.rem(z + d + NZ, NZ)

    def xr(d):
        return lax.rem(x + d + NX, NX)

    exchange = [send(exs.at[a], exr.at[a], partner) for a in range(2)]
    k0, k1 = 2 * c, 2 * c + 1

    q0x, q1z, q1x = [], [], [None, None]
    passed = [[[], []], [[], []]]

    def forward(a, q, ref):
        passed[a][q].append(send(ref, ref, partner))

    def build(a):
        exchange[a].wait_recv()
        mine = rows_in[a, :, pl.ds(pl.multiple_of(c * HW, HW), HW)].astype(F32)
        theirs = exr[a]
        first = jnp.where(c == 0, mine, theirs)
        second = jnp.where(c == 0, theirs, mine)
        rows = jnp.concatenate([first, second], axis=0).astype(BF16)
        xk[a, k0, z, x] = rows[:, :QW]
        xk[a, k1, z, x] = rows[:, QW:]
        here = xk.at[a, k0, z, x]
        q0x.append([send(here, here, at(dx=d)) for d in (1, 3, 2)])

    def over_z(a):
        here = xk.at[a, k1, z, x]
        q1z.append([send(here, here, at(dz=d)) for d in (1, 7, 2, 6, 3, 5, 4)])

    def over_x(a):
        for copy in q1z[a]:
            copy.wait_recv()
        here = xk.at[a, k1, :, x]
        q1x[a] = [send(here, here, at(dx=d)) for d in (1, 3, 2)]
        forward(a, 1, here)

    def over_x_done(a):
        for copy, d in zip(q1x[a], (1, 3, 2)):
            copy.wait_recv()
            forward(a, 1, xk.at[a, k1, :, xr(-d)])

    ring = [[[], []], [[], []]]

    def ring_start(a):
        for copy in q0x[a]:
            copy.wait_recv()
        here = xk.at[a, k0, z]
        ring[a][0].append(send(here, here, at(dz=1)))
        ring[a][1].append(send(here, here, at(dz=-1)))
        forward(a, 0, here)

    def ring_hop(a, hop):
        for side, sign in ((0, 1), (1, -1)):
            ring[a][side][hop - 1].wait_recv()
            got = xk.at[a, k0, zr(-sign * hop)]
            part = got
            if hop == 3:
                part = xk.at[a, k0, zr(-sign * hop), 2 * side : 2 * side + 2]
            ring[a][side].append(send(part, part, at(dz=sign)))
            forward(a, 0, got)

    def ring_done(a):
        for side in range(2):
            ring[a][side][3].wait_recv()
            forward(a, 0, xk.at[a, k0, zr(4), 2 * side : 2 * side + 2])

    def passed_on(a, q):
        for copy in passed[a][q]:
            copy.wait_recv()

    def spread_masks():
        feature_block = lax.broadcasted_iota(jnp.int32, (DL // BLOCK, DL), 1) // BLOCK
        block = lax.broadcasted_iota(jnp.int32, (DL // BLOCK, DL), 0)
        spread = (feature_block == block).astype(F32).astype(BF16)
        for i in range(3):
            loads[2 + i].wait()
            mx[i, 0 : FL // BLOCK] = jnp.dot(
                masks_in[i].astype(F32).astype(BF16), spread, preferred_element_type=F32
            )

    def prune(i):
        loads[5 + i].wait()

        @pl.loop(0, FL // BLOCK)
        def _(b):
            rows = pl.ds(pl.multiple_of(b * BLOCK, BLOCK), BLOCK)
            w[i, rows, :] = (w[i, rows, :].astype(F32) * mx[i, pl.ds(b, 1), :]).astype(BF16)

    def project(m, a, ks, last):
        @pl.loop(0, 4, unroll=True)
        def _(i):
            rows = pl.ds(pl.multiple_of((i // 2) * (FL // 2), FL // 2), FL // 2)
            cols = pl.ds(pl.multiple_of((i % 2) * 256, 256), 256)
            zs = pl.ds((i % 2) * 4, 4)
            total = pf[m, rows, cols] if len(ks) == 2 and last else None
            for k in ks:
                term = nt(
                    w[m, rows, k * QW : (k + 1) * QW],
                    xk[a, k, zs].reshape(256, QW),
                )
                total = term if total is None else total + term
            pf[m, rows, cols] = total
            if last:
                sb[m, rows, cols] = total.astype(BF16)

    def scatter(m):
        copies = []
        for d in (1, 3, 2):
            theirs = pl.ds(pl.multiple_of(lax.rem(f + d, NY) * SLAB, 16), SLAB)
            copies.append(send(sb.at[m, theirs, :], rb.at[m, d - 1], at(dy=d)))
        return copies

    build(0)
    spread_masks()
    ring_start(0)
    over_z(0)
    build(1)
    prune(0)
    ring_hop(0, 1)
    over_x(0)
    prune(1)
    ring_hop(0, 2)
    ring_start(1)
    ring_hop(0, 3)
    over_z(1)
    over_x_done(0)
    ring_hop(1, 1)
    passed_on(0, 1)
    project(0, 0, (1, 3), False)
    ring_done(0)
    passed_on(0, 0)
    project(0, 0, (0, 2), True)
    sums = [scatter(0)]
    over_x(1)
    ring_hop(1, 2)
    project(1, 0, (0, 1, 2, 3), True)
    sums.append(scatter(1))
    ring_hop(1, 3)
    prune(2)
    over_x_done(1)
    ring_done(1)
    passed_on(1, 0)
    passed_on(1, 1)
    project(2, 1, (0, 1, 2, 3), True)
    sums.append(scatter(2))

    my_slab = pl.multiple_of(f * SLAB, 16)
    def summed(m, b):
        rows = pl.ds(pl.multiple_of(b * 16, 16), 16)
        total = pf[m, pl.ds(pl.multiple_of(my_slab + b * 16, 16), 16), :]
        for d in range(3):
            total = total + rb[m, d, rows, :].astype(F32)
        return total

    def gather(i):
        here = full.at[i, pl.ds(my_slab, SLAB), :]
        return [send(here, here, at(dy=d)) for d in (1, -1)]

    def relay(i, near):
        copies = []
        for side, sign in ((0, 1), (1, -1)):
            near[side].wait_recv()
            rows = pl.ds(pl.multiple_of(lax.rem(f - sign + NY, NY) * SLAB, 16), SLAB)
            part = full.at[i, rows, pl.ds(side * (TOK // 2), TOK // 2)]
            copies.append(send(part, part, at(dy=sign)))
        return copies

    for m in range(2):
        for copy in sums[m]:
            copy.wait_recv()

    @pl.loop(0, SLAB // 16)
    def _(b):
        rows = pl.ds(pl.multiple_of(b * 16, 16), 16)
        gate = summed(0, b)
        upv = summed(1, b)
        sig = 1.0 / (1.0 + jnp.exp(-gate))
        activated = gate * sig
        full[0, pl.ds(pl.multiple_of(my_slab + b * 16, 16), 16), :] = (activated * upv).astype(BF16)
        act[0, rows, :] = activated
        act[1, rows, :] = upv * sig * (1.0 + gate * (1.0 - sig))

    near = [gather(0)]
    for copy in sums[2]:
        copy.wait_recv()

    @pl.loop(0, SLAB // 16)
    def _(b):
        rows = pl.ds(pl.multiple_of(b * 16, 16), 16)
        mine = pl.ds(pl.multiple_of(my_slab + b * 16, 16), 16)
        grad_hidden = summed(2, b)
        full[1, mine, :] = (grad_hidden * act[1, rows, :]).astype(BF16)
        full[2, mine, :] = (grad_hidden * act[0, rows, :]).astype(BF16)

    near.append(gather(1))
    far = [relay(0, near[0])]
    near.append(gather(2))
    far.append(relay(1, near[1]))

    def turn(i):
        @pl.loop(0, TOK // 128)
        def _(b):
            cols = pl.ds(pl.multiple_of(b * 128, 128), 128)
            tr[i, cols, :] = full[i, :, cols].astype(F32).T.astype(BF16)

    def product(a, pairs):
        copies = []
        for half, dst in ((o, psend), (c, own)):
            for step in range(2):
                j = lax.rem(z // 4 + 1 + step, 2)
                rows = pl.ds(pl.multiple_of(j * 256, 256), 256)
                zs = pl.ds(j * 4, 4)

                @pl.loop(0, HW // 256, unroll=True)
                def _(n):
                    cols = pl.ds(pl.multiple_of(half * HW + n * 256, 256), 256)
                    total = None
                    for i, m in pairs:
                        term = jnp.dot(
                            tr[i, rows, :], w[m, :, cols],
                            preferred_element_type=F32,
                        )
                        total = term if total is None else total + term
                    dst[a, zs, :, :, pl.ds(pl.multiple_of(n * 256, 256), 256)] = (
                        total.reshape(4, NX, 16, 256)
                    )

                if dst is psend:
                    copies.append(send(psend.at[a, zs], precv.at[a, zs], partner))
        return copies

    stores = []

    def weight_grad(i, a, m, dst, half):
        @pl.loop(2 * half, 2 * half + 2, unroll=True)
        def _(k):
            cols = pl.ds(pl.multiple_of(k * QW, QW), QW)
            total = jnp.dot(full[i], xk[a, k].reshape(TOK, QW), preferred_element_type=F32)
            for b in range(FL // BLOCK):
                rows = slice(b * BLOCK, (b + 1) * BLOCK)
                gout[m, rows, cols] = (total[rows] * mx[m, b : b + 1, cols]).astype(BF16)

        if half == 1:
            store = pltpu.make_async_copy(gout.at[m], dst, loc_sem.at[3 + m])
            store.start()
            stores.append(store)

    def part(a, zz, xs, q):
        cols = slice(q * QW, (q + 1) * QW)
        return own[a, zz, xs, :, cols] + precv[a, zz, xs, :, cols]

    swap, bulk, small, last, final = ([None, None] for _ in range(5))
    chain = [[[], []], [[], []]]

    def reduce_start(a):
        swap[a][0].wait_recv()
        for side, sign in ((0, 1), (1, -1)):
            ring_s[a, side, 0, 0:2] = part(a, zr(4), slice(2 * side, 2 * side + 2), 0).astype(BF16)
            chain[a][side].append(
                send(ring_s.at[a, side, 0, 0:2], ring_r.at[a, side, 0, 0:2], at(dz=sign))
            )
        swap[a][1].wait_recv()
        bulk[a] = []
        for d in (2, 1, 3):
            xsend[a, d - 1] = part(a, slice(0, NZ), xr(d), 1).astype(BF16)
            bulk[a].append(send(xsend.at[a, d - 1], xrecv.at[a, d - 1], at(dx=d)))

    def reduce_hop(a, hop):
        for side, sign in ((0, 1), (1, -1)):
            chain[a][side][hop - 1].wait_recv()
            to = zr(sign * (4 - hop))
            if hop == 1:
                lo, hi = slice(2 * side, 2 * side + 2), slice(2 - 2 * side, 4 - 2 * side)
                ring_s[a, side, hop, lo] = (
                    part(a, to, lo, 0) + ring_r[a, side, 0, 0:2].astype(F32)
                ).astype(BF16)
                ring_s[a, side, hop, hi] = part(a, to, hi, 0).astype(BF16)
            else:
                ring_s[a, side, hop] = (
                    part(a, to, slice(0, 4), 0) + ring_r[a, side, hop - 1].astype(F32)
                ).astype(BF16)
            chain[a][side].append(
                send(ring_s.at[a, side, hop], ring_r.at[a, side, hop], at(dz=sign))
            )

    def reduce_small(a):
        for copy in bulk[a]:
            copy.wait_recv()
        total = part(a, slice(0, NZ), x, 1)
        for d in range(3):
            total = total + xrecv[a, d].astype(F32)
        r1[a] = total
        small[a] = []
        for d in (4, 3, 5, 2, 6, 1, 7):
            zsend[a, d - 1] = r1[a, zr(d)].astype(BF16)
            small[a].append(send(zsend.at[a, d - 1], zrecv.at[a, d - 1], at(dz=d)))

    def reduce_last(a):
        for side in range(2):
            chain[a][side][3].wait_recv()
        r0[a] = part(a, z, slice(0, 4), 0) + ring_r[a, 0, 3].astype(F32) + ring_r[a, 1, 3].astype(F32)
        last[a] = []
        for d in (2, 1, 3):
            x2send[a, d - 1] = r0[a, xr(d)].astype(BF16)
            last[a].append(send(x2send.at[a, d - 1], x2recv.at[a, d - 1], at(dx=d)))

    def reduce_final(a):
        for copy in small[a]:
            copy.wait_recv()
        total1 = r1[a, z]
        for d in range(7):
            total1 = total1 + zrecv[a, d].astype(F32)
        fin[a, :, :, QW:] = total1.reshape(2, 8, QW)
        for copy in last[a]:
            copy.wait_recv()
        total0 = r0[a, x]
        for d in range(3):
            total0 = total0 + x2recv[a, d].astype(F32)
        fin[a, :, :, :QW] = total0.reshape(2, 8, QW)
        final[a] = send(fin.at[a, o], finr.at[a], partner)

    for copy in far[0]:
        copy.wait_recv()
    turn(0)
    swap[0] = product(0, ((0, 2),))
    far.append(relay(2, near[2]))
    reduce_start(0)
    weight_grad(0, 1, 2, gd_hbm, 0)
    weight_grad(0, 1, 2, gd_hbm, 1)
    reduce_hop(0, 1)
    for i in range(2):
        for copy in far[1 + i]:
            copy.wait_recv()
        turn(1 + i)
    swap[1] = product(1, ((1, 0), (2, 1)))
    reduce_start(1)
    reduce_hop(0, 2)
    reduce_small(0)
    reduce_hop(1, 1)
    weight_grad(1, 0, 0, gg_hbm, 0)
    reduce_hop(0, 3)
    reduce_hop(1, 2)
    weight_grad(1, 0, 0, gg_hbm, 1)
    reduce_last(0)
    reduce_small(1)
    reduce_hop(1, 3)
    weight_grad(2, 0, 1, gu_hbm, 0)
    reduce_final(0)
    reduce_last(1)
    weight_grad(2, 0, 1, gu_hbm, 1)
    reduce_final(1)
    for a, ref in enumerate((out_ref, gtok_ref)):
        final[a].wait_recv()
        ref[:, pl.ds(pl.multiple_of(c * HW, HW), HW)] = fin[a, c].astype(BF16)
        ref[:, pl.ds(pl.multiple_of(o * HW, HW), HW)] = finr[a].astype(BF16)

    for copy in sent:
        copy.wait_send()
    for store in stores:
        store.wait()


def deliver(*refs):
    srcs, dsts, bufs, (in_sem, out_sem) = refs[:5], refs[5:10], refs[10:15], refs[15:]
    steps = []
    for i in range(5):
        load = pltpu.make_async_copy(srcs[i], bufs[i], in_sem.at[i])
        load.start()
        steps.append((load, pltpu.make_async_copy(bufs[i], dsts[i], out_sem.at[i])))
    for load, store in steps:
        load.wait()
        store.start()
    for _, store in steps:
        store.wait()


def body(tokens, gate_weight, up_weight, down_weight, gate_mask, up_mask, down_mask, grad_out):
    vmem = pl.BlockSpec(memory_space=pltpu.VMEM)
    hbm = pl.BlockSpec(memory_space=pl.ANY)
    out, gtok, gg, gu, gd = pl.pallas_call(
        kernel,
        name="ffn",
        out_shape=(
            jax.ShapeDtypeStruct((8, DL), BF16),
            jax.ShapeDtypeStruct((8, DL), BF16),
            jax.ShapeDtypeStruct((FL, DL), BF16),
            jax.ShapeDtypeStruct((FL, DL), BF16),
            jax.ShapeDtypeStruct((FL, DL), BF16),
        ),
        in_specs=[hbm] * 8,
        out_specs=(vmem, vmem, hbm, hbm, hbm),
        scratch_shapes=[
            pltpu.VMEM((2, 8, DL), BF16),
            pltpu.VMEM((3, FL // BLOCK, DL // BLOCK), jnp.int32),
            pltpu.VMEM((3, FL, DL), BF16),
            pltpu.VMEM((3, 8, DL), F32),
            pltpu.VMEM((2, 4, NZ, NX, 16, QW), BF16),
            pltpu.VMEM((2, 8, HW), F32),
            pltpu.VMEM((2, 8, HW), F32),
            pltpu.VMEM((3, FL, TOK), F32),
            pltpu.VMEM((3, FL, TOK), BF16),
            pltpu.VMEM((3, 3, SLAB, TOK), BF16),
            pltpu.VMEM((2, SLAB, TOK), F32),
            pltpu.VMEM((3, FL, TOK), BF16),
            pltpu.VMEM((3, TOK, FL), BF16),
            pltpu.VMEM((2, NZ, NX, 16, HW), F32),
            pltpu.VMEM((2, NZ, NX, 16, HW), F32),
            pltpu.VMEM((2, NZ, NX, 16, HW), F32),
            pltpu.VMEM((2, 3, NZ, 16, QW), BF16),
            pltpu.VMEM((2, 3, NZ, 16, QW), BF16),
            pltpu.VMEM((2, 3, 16, QW), BF16),
            pltpu.VMEM((2, 3, 16, QW), BF16),
            pltpu.VMEM((2, 2, 4, NX, 16, QW), BF16),
            pltpu.VMEM((2, 2, 4, NX, 16, QW), BF16),
            pltpu.VMEM((2, NX, 16, QW), F32),
            pltpu.VMEM((2, NZ, 16, QW), F32),
            pltpu.VMEM((2, 7, 16, QW), BF16),
            pltpu.VMEM((2, 7, 16, QW), BF16),
            pltpu.VMEM((2, 2, 8, HW), F32),
            pltpu.VMEM((2, 8, HW), F32),
            pltpu.VMEM((3, FL, DL), BF16),
            pltpu.SemaphoreType.DMA((N_SEMS,)),
            pltpu.SemaphoreType.DMA((N_SEMS,)),
            pltpu.SemaphoreType.DMA((11,)),
        ],
        compiler_params=pltpu.CompilerParams(
            collective_id=0, has_side_effects=True, vmem_limit_bytes=VMEM
        ),
    )(
        tokens, grad_out, gate_weight.T, up_weight.T, down_weight,
        gate_mask.T, up_mask.T, down_mask,
    )
    results = (out, gtok, gg, gu, gd)
    out, gtok, gg, gu, gd = pl.pallas_call(
        deliver,
        name="deliver",
        out_shape=tuple(jax.ShapeDtypeStruct(r.shape, r.dtype) for r in results),
        in_specs=[hbm] * 5,
        out_specs=(hbm,) * 5,
        scratch_shapes=[pltpu.VMEM(r.shape, r.dtype) for r in results]
        + [pltpu.SemaphoreType.DMA((5,)), pltpu.SemaphoreType.DMA((5,))],
        compiler_params=pltpu.CompilerParams(vmem_limit_bytes=VMEM),
    )(*results)
    return out, gtok, gg.T, gu.T, gd


def solution(mesh):
    placed = (
        P("tp", "fsdp"),
        P("fsdp", "tp"),
        P("fsdp", "tp"),
        P("tp", "fsdp"),
        P("fsdp", "tp"),
        P("fsdp", "tp"),
        P("tp", "fsdp"),
        P("tp", "fsdp"),
    )
    return jax.shard_map(
        body,
        mesh=mesh,
        in_specs=placed,
        out_specs=(
            P("tp", "fsdp"),
            P("tp", "fsdp"),
            P("fsdp", "tp"),
            P("fsdp", "tp"),
            P("tp", "fsdp"),
        ),
        check_vma=False,
    )
```

```python
import jax
import jax.numpy as jnp
from jax import lax
from jax.experimental import pallas as pl
from jax.experimental.pallas import tpu as pltpu
from jax.sharding import PartitionSpec as P

NY, NZ, NX = 4, 8, 4
BLOCK = 64
TOK = 512
DL = 2048
FL = 448
SLAB = FL // NY
QW = DL // 4
HW = DL // 2
F32 = jnp.float32
BF16 = jnp.bfloat16
MESH = pl.DeviceIdType.MESH
N_SEMS = 160
VMEM = 57 * 2**20


def nt(left, right):
    return lax.dot_general(left, right, (((1,), (1,)), ((), ())), preferred_element_type=F32)


def kernel(
    tok_hbm, cot_hbm, wg_hbm, wu_hbm, wd_hbm, mg_hbm, mu_hbm, md_hbm,
    out_ref, gtok_ref, gg_hbm, gu_hbm, gd_hbm,
    rows_in, masks_in, w, mx, xk, exs, exr, pf, sb, rb, act, full, tr,
    own, psend, precv, xsend, xrecv, x2send, x2recv, ring_s, ring_r,
    r0, r1, zsend, zrecv, fin, finr, gout,
    send_sem, recv_sem, loc_sem,
):
    f = lax.axis_index("fsdp")
    t = lax.axis_index("tp")
    z = t // (2 * NX)
    x = (t // 2) % NX
    c = t % 2
    o = 1 - c

    def at(dy=0, dz=0, dx=0, flip=False):
        core = o if flip else c
        zz = lax.rem(z + dz + NZ, NZ)
        xx = lax.rem(x + dx + NX, NX)
        return (lax.rem(f + dy + NY, NY), zz * (2 * NX) + xx * 2 + core)

    partner = at(flip=True)
    peers = [at(dy=d) for d in range(1, NY)]
    peers += [at(dz=d) for d in range(1, NZ)]
    peers += [at(dx=d) for d in range(1, NX)]
    peers += [partner]

    barrier = pltpu.get_barrier_semaphore()
    for peer in peers:
        pl.semaphore_signal(barrier, inc=1, device_id=peer, device_id_type=MESH)

    tokens_in = [
        pltpu.make_async_copy(src, rows_in.at[a], loc_sem.at[6 + a])
        for a, src in enumerate((tok_hbm, cot_hbm))
    ]
    blocks_in = [
        pltpu.make_async_copy(src, masks_in.at[i], loc_sem.at[8 + i])
        for i, src in enumerate((mg_hbm, mu_hbm, md_hbm))
    ]
    loads = [
        pltpu.make_async_copy(src, w.at[i], loc_sem.at[i])
        for i, src in enumerate((wg_hbm, wu_hbm, wd_hbm))
    ]
    loads = tokens_in + blocks_in + loads
    for load in loads:
        load.start()

    for a in range(2):
        loads[a].wait()
        exs[a] = rows_in[a, :, pl.ds(pl.multiple_of(o * HW, HW), HW)].astype(F32)
    pl.semaphore_wait(barrier, len(peers))

    sent = []

    def send(src, dst, peer):
        i = len(sent)
        copy = pltpu.make_async_remote_copy(
            src_ref=src, dst_ref=dst, send_sem=send_sem.at[i], recv_sem=recv_sem.at[i],
            device_id=peer, device_id_type=MESH,
        )
        copy.start()
        sent.append(copy)
        return copy

    def zr(d):
        return lax.rem(z + d + NZ, NZ)

    def xr(d):
        return lax.rem(x + d + NX, NX)

    exchange = [send(exs.at[a], exr.at[a], partner) for a in range(2)]
    k0, k1 = 2 * c, 2 * c + 1

    q0x, q1z, q1x = [], [], [None, None]
    passed = [[[], []], [[], []]]

    def forward(a, q, ref):
        passed[a][q].append(send(ref, ref, partner))

    def build(a):
        exchange[a].wait_recv()
        mine = rows_in[a, :, pl.ds(pl.multiple_of(c * HW, HW), HW)].astype(F32)
        theirs = exr[a]
        first = jnp.where(c == 0, mine, theirs)
        second = jnp.where(c == 0, theirs, mine)
        rows = jnp.concatenate([first, second], axis=0).astype(BF16)
        xk[a, k0, z, x] = rows[:, :QW]
        xk[a, k1, z, x] = rows[:, QW:]
        here = xk.at[a, k0, z, x]
        q0x.append([send(here, here, at(dx=d)) for d in (1, 3, 2)])

    def over_z(a):
        here = xk.at[a, k1, z, x]
        q1z.append([send(here, here, at(dz=d)) for d in (1, 7, 2, 6, 3, 5, 4)])

    def over_x(a):
        for copy in q1z[a]:
            copy.wait_recv()
        here = xk.at[a, k1, :, x]
        q1x[a] = [send(here, here, at(dx=d)) for d in (1, 3, 2)]
        forward(a, 1, here)

    def over_x_done(a):
        for copy, d in zip(q1x[a], (1, 3, 2)):
            copy.wait_recv()
            forward(a, 1, xk.at[a, k1, :, xr(-d)])

    ring = [[[], []], [[], []]]

    def ring_start(a):
        for copy in q0x[a]:
            copy.wait_recv()
        here = xk.at[a, k0, z]
        ring[a][0].append(send(here, here, at(dz=1)))
        ring[a][1].append(send(here, here, at(dz=-1)))
        forward(a, 0, here)

    def ring_hop(a, hop):
        for side, sign in ((0, 1), (1, -1)):
            ring[a][side][hop - 1].wait_recv()
            got = xk.at[a, k0, zr(-sign * hop)]
            part = got
            if hop == 3:
                part = xk.at[a, k0, zr(-sign * hop), 2 * side : 2 * side + 2]
            ring[a][side].append(send(part, part, at(dz=sign)))
            forward(a, 0, got)

    def ring_done(a):
        for side in range(2):
            ring[a][side][3].wait_recv()
            forward(a, 0, xk.at[a, k0, zr(4), 2 * side : 2 * side + 2])

    def passed_on(a, q):
        for copy in passed[a][q]:
            copy.wait_recv()

    def spread_masks():
        feature_block = lax.broadcasted_iota(jnp.int32, (DL // BLOCK, DL), 1) // BLOCK
        block = lax.broadcasted_iota(jnp.int32, (DL // BLOCK, DL), 0)
        spread = (feature_block == block).astype(F32).astype(BF16)
        for i in range(3):
            loads[2 + i].wait()
            mx[i, 0 : FL // BLOCK] = jnp.dot(
                masks_in[i].astype(F32).astype(BF16), spread, preferred_element_type=F32
            )

    def prune(i):
        loads[5 + i].wait()

        @pl.loop(0, FL // BLOCK)
        def _(b):
            rows = pl.ds(pl.multiple_of(b * BLOCK, BLOCK), BLOCK)
            w[i, rows, :] = (w[i, rows, :].astype(F32) * mx[i, pl.ds(b, 1), :]).astype(BF16)

    def project(m, a, ks, last):
        @pl.loop(0, 4, unroll=True)
        def _(i):
            rows = pl.ds(pl.multiple_of((i // 2) * (FL // 2), FL // 2), FL // 2)
            cols = pl.ds(pl.multiple_of((i % 2) * 256, 256), 256)
            zs = pl.ds((i % 2) * 4, 4)
            total = pf[m, rows, cols] if len(ks) == 2 and last else None
            for k in ks:
                term = nt(
                    w[m, rows, k * QW : (k + 1) * QW],
                    xk[a, k, zs].reshape(256, QW),
                )
                total = term if total is None else total + term
            pf[m, rows, cols] = total
            if last:
                sb[m, rows, cols] = total.astype(BF16)

    def scatter(m):
        copies = []
        for d in (1, 3, 2):
            theirs = pl.ds(pl.multiple_of(lax.rem(f + d, NY) * SLAB, 16), SLAB)
            copies.append(send(sb.at[m, theirs, :], rb.at[m, d - 1], at(dy=d)))
        return copies

    build(0)
    spread_masks()
    ring_start(0)
    over_z(0)
    build(1)
    prune(0)
    ring_hop(0, 1)
    over_x(0)
    prune(1)
    ring_hop(0, 2)
    ring_start(1)
    ring_hop(0, 3)
    over_z(1)
    over_x_done(0)
    passed_on(0, 1)
    project(0, 0, (1, 3), False)
    ring_done(0)
    passed_on(0, 0)
    project(0, 0, (0, 2), True)
    sums = [scatter(0)]
    ring_hop(1, 1)
    over_x(1)
    ring_hop(1, 2)
    project(1, 0, (0, 1, 2, 3), True)
    sums.append(scatter(1))
    ring_hop(1, 3)
    prune(2)
    over_x_done(1)
    ring_done(1)
    passed_on(1, 0)
    passed_on(1, 1)
    project(2, 1, (0, 1, 2, 3), True)
    sums.append(scatter(2))

    my_slab = pl.multiple_of(f * SLAB, 16)
    def summed(m, b):
        rows = pl.ds(pl.multiple_of(b * 16, 16), 16)
        total = pf[m, pl.ds(pl.multiple_of(my_slab + b * 16, 16), 16), :]
        for d in range(3):
            total = total + rb[m, d, rows, :].astype(F32)
        return total

    def gather(i):
        here = full.at[i, pl.ds(my_slab, SLAB), :]
        return [send(here, here, at(dy=d)) for d in (1, -1)]

    def relay(i, near):
        copies = []
        for side, sign in ((0, 1), (1, -1)):
            near[side].wait_recv()
            rows = pl.ds(pl.multiple_of(lax.rem(f - sign + NY, NY) * SLAB, 16), SLAB)
            part = full.at[i, rows, pl.ds(side * (TOK // 2), TOK // 2)]
            copies.append(send(part, part, at(dy=sign)))
        return copies

    for m in range(2):
        for copy in sums[m]:
            copy.wait_recv()

    @pl.loop(0, SLAB // 16)
    def _(b):
        rows = pl.ds(pl.multiple_of(b * 16, 16), 16)
        gate = summed(0, b)
        upv = summed(1, b)
        sig = 1.0 / (1.0 + jnp.exp(-gate))
        activated = gate * sig
        full[0, pl.ds(pl.multiple_of(my_slab + b * 16, 16), 16), :] = (activated * upv).astype(BF16)
        act[0, rows, :] = activated
        act[1, rows, :] = upv * sig * (1.0 + gate * (1.0 - sig))

    near = [gather(0)]
    for copy in sums[2]:
        copy.wait_recv()

    @pl.loop(0, SLAB // 16)
    def _(b):
        rows = pl.ds(pl.multiple_of(b * 16, 16), 16)
        mine = pl.ds(pl.multiple_of(my_slab + b * 16, 16), 16)
        grad_hidden = summed(2, b)
        full[1, mine, :] = (grad_hidden * act[1, rows, :]).astype(BF16)
        full[2, mine, :] = (grad_hidden * act[0, rows, :]).astype(BF16)

    near.append(gather(1))
    far = [relay(0, near[0])]
    near.append(gather(2))
    far.append(relay(1, near[1]))

    def turn(i):
        @pl.loop(0, TOK // 128)
        def _(b):
            cols = pl.ds(pl.multiple_of(b * 128, 128), 128)
            tr[i, cols, :] = full[i, :, cols].astype(F32).T.astype(BF16)

    def product(a, pairs):
        copies = []
        for half, dst in ((o, psend), (c, own)):
            for step in range(2):
                j = lax.rem(z // 4 + 1 + step, 2)
                rows = pl.ds(pl.multiple_of(j * 256, 256), 256)
                zs = pl.ds(j * 4, 4)

                @pl.loop(0, HW // 256, unroll=True)
                def _(n):
                    cols = pl.ds(pl.multiple_of(half * HW + n * 256, 256), 256)
                    total = None
                    for i, m in pairs:
                        term = jnp.dot(
                            tr[i, rows, :], w[m, :, cols],
                            preferred_element_type=F32,
                        )
                        total = term if total is None else total + term
                    dst[a, zs, :, :, pl.ds(pl.multiple_of(n * 256, 256), 256)] = (
                        total.reshape(4, NX, 16, 256)
                    )

                if dst is psend:
                    copies.append(send(psend.at[a, zs], precv.at[a, zs], partner))
        return copies

    stores = []

    def weight_grad(i, a, m, dst, half):
        @pl.loop(2 * half, 2 * half + 2, unroll=True)
        def _(k):
            cols = pl.ds(pl.multiple_of(k * QW, QW), QW)
            total = jnp.dot(full[i], xk[a, k].reshape(TOK, QW), preferred_element_type=F32)
            for b in range(FL // BLOCK):
                rows = slice(b * BLOCK, (b + 1) * BLOCK)
                gout[m, rows, cols] = (total[rows] * mx[m, b : b + 1, cols]).astype(BF16)

        if half == 1:
            store = pltpu.make_async_copy(gout.at[m], dst, loc_sem.at[3 + m])
            store.start()
            stores.append(store)

    def part(a, zz, xs, q):
        cols = slice(q * QW, (q + 1) * QW)
        return own[a, zz, xs, :, cols] + precv[a, zz, xs, :, cols]

    swap, bulk, small, last, final = ([None, None] for _ in range(5))
    chain = [[[], []], [[], []]]

    def reduce_start(a):
        swap[a][0].wait_recv()
        for side, sign in ((0, 1), (1, -1)):
            ring_s[a, side, 0, 0:2] = part(a, zr(4), slice(2 * side, 2 * side + 2), 0).astype(BF16)
            chain[a][side].append(
                send(ring_s.at[a, side, 0, 0:2], ring_r.at[a, side, 0, 0:2], at(dz=sign))
            )
        swap[a][1].wait_recv()
        bulk[a] = []
        for d in (2, 1, 3):
            xsend[a, d - 1] = part(a, slice(0, NZ), xr(d), 1).astype(BF16)
            bulk[a].append(send(xsend.at[a, d - 1], xrecv.at[a, d - 1], at(dx=d)))

    def reduce_hop(a, hop):
        for side, sign in ((0, 1), (1, -1)):
            chain[a][side][hop - 1].wait_recv()
            to = zr(sign * (4 - hop))
            if hop == 1:
                lo, hi = slice(2 * side, 2 * side + 2), slice(2 - 2 * side, 4 - 2 * side)
                ring_s[a, side, hop, lo] = (
                    part(a, to, lo, 0) + ring_r[a, side, 0, 0:2].astype(F32)
                ).astype(BF16)
                ring_s[a, side, hop, hi] = part(a, to, hi, 0).astype(BF16)
            else:
                ring_s[a, side, hop] = (
                    part(a, to, slice(0, 4), 0) + ring_r[a, side, hop - 1].astype(F32)
                ).astype(BF16)
            chain[a][side].append(
                send(ring_s.at[a, side, hop], ring_r.at[a, side, hop], at(dz=sign))
            )

    def reduce_small(a):
        for copy in bulk[a]:
            copy.wait_recv()
        total = part(a, slice(0, NZ), x, 1)
        for d in range(3):
            total = total + xrecv[a, d].astype(F32)
        r1[a] = total
        small[a] = []
        for d in (4, 3, 5, 2, 6, 1, 7):
            zsend[a, d - 1] = r1[a, zr(d)].astype(BF16)
            small[a].append(send(zsend.at[a, d - 1], zrecv.at[a, d - 1], at(dz=d)))

    def reduce_last(a):
        for side in range(2):
            chain[a][side][3].wait_recv()
        r0[a] = part(a, z, slice(0, 4), 0) + ring_r[a, 0, 3].astype(F32) + ring_r[a, 1, 3].astype(F32)
        last[a] = []
        for d in (2, 1, 3):
            x2send[a, d - 1] = r0[a, xr(d)].astype(BF16)
            last[a].append(send(x2send.at[a, d - 1], x2recv.at[a, d - 1], at(dx=d)))

    def reduce_final(a):
        for copy in small[a]:
            copy.wait_recv()
        total1 = r1[a, z]
        for d in range(7):
            total1 = total1 + zrecv[a, d].astype(F32)
        fin[a, :, :, QW:] = total1.reshape(2, 8, QW)
        for copy in last[a]:
            copy.wait_recv()
        total0 = r0[a, x]
        for d in range(3):
            total0 = total0 + x2recv[a, d].astype(F32)
        fin[a, :, :, :QW] = total0.reshape(2, 8, QW)
        final[a] = send(fin.at[a, o], finr.at[a], partner)

    for copy in far[0]:
        copy.wait_recv()
    turn(0)
    swap[0] = product(0, ((0, 2),))
    far.append(relay(2, near[2]))
    reduce_start(0)
    weight_grad(0, 1, 2, gd_hbm, 0)
    weight_grad(0, 1, 2, gd_hbm, 1)
    reduce_hop(0, 1)
    for copy in far[1]:
        copy.wait_recv()
    turn(1)
    weight_grad(1, 0, 0, gg_hbm, 0)
    weight_grad(1, 0, 0, gg_hbm, 1)
    for copy in far[2]:
        copy.wait_recv()
    turn(2)
    swap[1] = product(1, ((1, 0), (2, 1)))
    reduce_start(1)
    reduce_hop(0, 2)
    reduce_small(0)
    reduce_hop(1, 1)
    reduce_hop(0, 3)
    reduce_hop(1, 2)
    reduce_last(0)
    reduce_small(1)
    reduce_hop(1, 3)
    weight_grad(2, 0, 1, gu_hbm, 0)
    reduce_final(0)
    reduce_last(1)
    weight_grad(2, 0, 1, gu_hbm, 1)
    reduce_final(1)
    for a, ref in enumerate((out_ref, gtok_ref)):
        final[a].wait_recv()
        ref[:, pl.ds(pl.multiple_of(c * HW, HW), HW)] = fin[a, c].astype(BF16)
        ref[:, pl.ds(pl.multiple_of(o * HW, HW), HW)] = finr[a].astype(BF16)

    for copy in sent:
        copy.wait_send()
    for store in stores:
        store.wait()


def deliver(*refs):
    srcs, dsts, bufs, (in_sem, out_sem) = refs[:5], refs[5:10], refs[10:15], refs[15:]
    steps = []
    for i in range(5):
        load = pltpu.make_async_copy(srcs[i], bufs[i], in_sem.at[i])
        load.start()
        steps.append((load, pltpu.make_async_copy(bufs[i], dsts[i], out_sem.at[i])))
    for load, store in steps:
        load.wait()
        store.start()
    for _, store in steps:
        store.wait()


def body(tokens, gate_weight, up_weight, down_weight, gate_mask, up_mask, down_mask, grad_out):
    vmem = pl.BlockSpec(memory_space=pltpu.VMEM)
    hbm = pl.BlockSpec(memory_space=pl.ANY)
    out, gtok, gg, gu, gd = pl.pallas_call(
        kernel,
        name="ffn",
        out_shape=(
            jax.ShapeDtypeStruct((8, DL), BF16),
            jax.ShapeDtypeStruct((8, DL), BF16),
            jax.ShapeDtypeStruct((FL, DL), BF16),
            jax.ShapeDtypeStruct((FL, DL), BF16),
            jax.ShapeDtypeStruct((FL, DL), BF16),
        ),
        in_specs=[hbm] * 8,
        out_specs=(vmem, vmem, hbm, hbm, hbm),
        scratch_shapes=[
            pltpu.VMEM((2, 8, DL), BF16),
            pltpu.VMEM((3, FL // BLOCK, DL // BLOCK), jnp.int32),
            pltpu.VMEM((3, FL, DL), BF16),
            pltpu.VMEM((3, 8, DL), F32),
            pltpu.VMEM((2, 4, NZ, NX, 16, QW), BF16),
            pltpu.VMEM((2, 8, HW), F32),
            pltpu.VMEM((2, 8, HW), F32),
            pltpu.VMEM((3, FL, TOK), F32),
            pltpu.VMEM((3, FL, TOK), BF16),
            pltpu.VMEM((3, 3, SLAB, TOK), BF16),
            pltpu.VMEM((2, SLAB, TOK), F32),
            pltpu.VMEM((3, FL, TOK), BF16),
            pltpu.VMEM((3, TOK, FL), BF16),
            pltpu.VMEM((2, NZ, NX, 16, HW), F32),
            pltpu.VMEM((2, NZ, NX, 16, HW), F32),
            pltpu.VMEM((2, NZ, NX, 16, HW), F32),
            pltpu.VMEM((2, 3, NZ, 16, QW), BF16),
            pltpu.VMEM((2, 3, NZ, 16, QW), BF16),
            pltpu.VMEM((2, 3, 16, QW), BF16),
            pltpu.VMEM((2, 3, 16, QW), BF16),
            pltpu.VMEM((2, 2, 4, NX, 16, QW), BF16),
            pltpu.VMEM((2, 2, 4, NX, 16, QW), BF16),
            pltpu.VMEM((2, NX, 16, QW), F32),
            pltpu.VMEM((2, NZ, 16, QW), F32),
            pltpu.VMEM((2, 7, 16, QW), BF16),
            pltpu.VMEM((2, 7, 16, QW), BF16),
            pltpu.VMEM((2, 2, 8, HW), F32),
            pltpu.VMEM((2, 8, HW), F32),
            pltpu.VMEM((3, FL, DL), BF16),
            pltpu.SemaphoreType.DMA((N_SEMS,)),
            pltpu.SemaphoreType.DMA((N_SEMS,)),
            pltpu.SemaphoreType.DMA((11,)),
        ],
        compiler_params=pltpu.CompilerParams(
            collective_id=0, has_side_effects=True, vmem_limit_bytes=VMEM
        ),
    )(
        tokens, grad_out, gate_weight.T, up_weight.T, down_weight,
        gate_mask.T, up_mask.T, down_mask,
    )
    results = (out, gtok, gg, gu, gd)
    out, gtok, gg, gu, gd = pl.pallas_call(
        deliver,
        name="deliver",
        out_shape=tuple(jax.ShapeDtypeStruct(r.shape, r.dtype) for r in results),
        in_specs=[hbm] * 5,
        out_specs=(hbm,) * 5,
        scratch_shapes=[pltpu.VMEM(r.shape, r.dtype) for r in results]
        + [pltpu.SemaphoreType.DMA((5,)), pltpu.SemaphoreType.DMA((5,))],
        compiler_params=pltpu.CompilerParams(vmem_limit_bytes=VMEM),
    )(*results)
    return out, gtok, gg.T, gu.T, gd


def solution(mesh):
    placed = (
        P("tp", "fsdp"),
        P("fsdp", "tp"),
        P("fsdp", "tp"),
        P("tp", "fsdp"),
        P("fsdp", "tp"),
        P("fsdp", "tp"),
        P("tp", "fsdp"),
        P("tp", "fsdp"),
    )
    return jax.shard_map(
        body,
        mesh=mesh,
        in_specs=placed,
        out_specs=(
            P("tp", "fsdp"),
            P("tp", "fsdp"),
            P("fsdp", "tp"),
            P("fsdp", "tp"),
            P("tp", "fsdp"),
        ),
        check_vma=False,
    )
```
